32 devices in a mesh: seq: 8 (over z, y), tp: 4 (over x, core).
Axes of the slice: x: 2, y: 2, z: 4, core: 2. Of those that a mesh axis runs over, the one named last changes fastest.
Arguments:
- tokens: bfloat16 [1024, 2048], P('seq'), may hold values from -6 to 6
- norm_gain: float32 [2048], replicated, may hold values from 0.5 to 1.5
- w_x: bfloat16 [2048, 2048], P(None, 'tp'), may hold values from -0.125 to 0.125
- w_z: bfloat16 [2048, 2048], P(None, 'tp'), may hold values from -0.125 to 0.125
- conv_w: float32 [4, 2048], P(None, 'tp'), may hold values from -3 to 3
- conv_b: float32 [2048], P('tp'), may hold values from -0.5 to 0.5
- w_xproj: bfloat16 [2048, 160], P('tp'), may hold values from -0.125 to 0.125
- w_dt: bfloat16 [128, 2048], P(None, 'tp'), may hold values from -0.5 to 0.5
- dt_bias: float32 [2048], P('tp'), may hold values from -4.6 to -3.4
- a_log: float32 [16, 2048], P(None, 'tp'), may hold values from -3.9 to -0.7
- d_skip: float32 [2048], P('tp'), may hold values from 0.5 to 1.5
- w_out: bfloat16 [2048, 2048], P('tp'), may hold values from -0.125 to 0.125
- mlp_gain: float32 [2048], replicated, may hold values from 0.5 to 1.5
- w_gate: bfloat16 [2048, 4096], P(None, 'tp'), may hold values from -0.125 to 0.125
- w_up: bfloat16 [2048, 4096], P(None, 'tp'), may hold values from -0.125 to 0.125
- w_down: bfloat16 [4096, 2048], P('tp'), may hold values from -0.09375 to 0.09375
- prompt_lengths: int32 [4], replicated, may hold values from 1 to 512, as said below
- request_prompt: int32 [32], P('seq'), may hold values from 0 to 3, as said below
Outputs:
- mixed_out: bfloat16 [1024, 2048], P(('seq', 'tp'))
- req_states: float32 [32, 16, 2048], P('seq', None, 'tp')
- req_edges: bfloat16 [32, 3, 2048], P('seq', None, 'tp')
The draws below stay inside these ranges and needn't reach their ends.
Inputs may be any that keep to these rules, and one draw needn't show every extreme that they name: `prompt_lengths`: the prompts are packed in order from slot 0 and sum to 960 tokens; the remaining slots are padding; the last prompt is exactly 512 long. `request_prompt`: every prompt is continued by at least one request.
All inputs are finite; a program needn't handle non-finite values.
Results may differ from the reference program's by a relative error of at most 0.025.
Values may be sent and summed in bfloat16 or wider, within the bound.
A program may use at most 128 MiB of HBM per device.

```python
import jax
import jax.numpy as jnp
from jax import lax

D = 2048
E = 2048
N = 16
K = 4
R = 128
FF = 4096
BLOCK = 128
TOKENS = 1024
PROMPTS = 4
LEN_MAX = 512
REQ = 32
N_TP = 4


def draw_prompt_lengths(key, part):
    total_len = TOKENS - BLOCK // 2
    key_order, key_weight = jax.random.split(jax.random.fold_in(key, 3), 2)
    shuffled = jax.random.permutation(key_order, PROMPTS).astype(jnp.int32)
    long_index = PROMPTS - 1
    short_index = jnp.where(shuffled[0] == long_index, shuffled[1], shuffled[0])
    prompt_ids = jnp.arange(PROMPTS, dtype=jnp.int32)
    others = (prompt_ids != long_index) & (prompt_ids != short_index)
    weights = jnp.where(others, jax.random.randint(key_weight, (PROMPTS,), 1, 5, dtype=jnp.int32), 0)
    spread_left = total_len - LEN_MAX - 1 - (PROMPTS - 2)
    shares = spread_left * weights // jnp.sum(weights)
    leftover = spread_left - jnp.sum(shares)
    rank_among = jnp.cumsum(others.astype(jnp.int32)) - 1
    extra_one = (others & (rank_among < leftover)).astype(jnp.int32)
    lengths = jnp.where(others, 1 + shares + extra_one, 0)
    lengths = lengths + jnp.where(prompt_ids == long_index, LEN_MAX, 0) + jnp.where(prompt_ids == short_index, 1, 0)
    return lengths.astype(jnp.int32)


def draw_request_prompt(key, part):
    key_pick, key_place = jax.random.split(jax.random.fold_in(key, 7), 2)
    picked = jax.random.randint(key_pick, (REQ,), 0, PROMPTS, dtype=jnp.int32)
    placed = jax.random.permutation(key_place, REQ)[:PROMPTS]
    return picked.at[placed].set(jnp.arange(PROMPTS, dtype=jnp.int32)).astype(jnp.int32)


def block_scale(stream_key, shape, cuts, least, high):
    def one(axis_at, shards_of):
        heights = jax.random.uniform(jax.random.fold_in(jax.random.fold_in(stream_key, 6), axis_at), (shards_of,), jnp.float32, least / len(cuts), high / len(cuts))
        return jnp.repeat(jnp.exp(heights), shape[axis_at] // shards_of).reshape((-1,) + (1,) * (len(shape) - axis_at - 1))

    level = one(*cuts[0])
    for cut in cuts[1:]:
        level = level * one(*cut)
    return level


def bell_draw(rng, dims, width, bound, cuts=(), kind=jnp.bfloat16):
    entries = width * jax.random.normal(rng, dims, jnp.float32)
    if cuts:
        entries = entries * block_scale(rng, dims, cuts, -0.22, 0.18)
    return jnp.clip(entries, -bound, bound).astype(kind)


def setup_inputs(seed: int = 0) -> dict:
    splits = jax.random.split(jax.random.key(seed), 19)
    tokens = bell_draw(splits[0], (TOKENS, D), 1.0, 6.0, ((0, 8),))
    norm_gain = jnp.clip(1.0 + 0.1 * jax.random.normal(splits[1], (D,), jnp.float32), 0.5, 1.5)
    w_x = bell_draw(splits[2], (D, E), D ** -0.5, 0.125, ((1, 4),))
    w_z = bell_draw(splits[3], (D, E), D ** -0.5, 0.125, ((1, 4),))
    conv_w = bell_draw(splits[4], (K, E), K ** -0.5, 3.0, ((1, 4),), jnp.float32)
    conv_b = jnp.clip(jax.random.uniform(splits[5], (E,), jnp.float32, -0.5, 0.5) * block_scale(splits[5], (E,), ((0, 4),), -0.4, 0.0), -0.5, 0.5)
    w_xproj = bell_draw(splits[6], (E, R + 2 * N), E ** -0.5, 0.125, ((0, 4),))
    w_dt = bell_draw(splits[7], (R, E), R ** -0.5, 0.5, ((1, 4),))
    dt_bias = jnp.clip(-4.6 + 1.1999998 * jax.random.uniform(splits[8], (E,), jnp.float32) ** block_scale(splits[8], (E,), ((0, 4),), -0.2, 0.2), -4.6, -3.4)
    a_log = jnp.clip(-3.9 + 3.2 * jax.random.uniform(splits[9], (N, E), jnp.float32) ** block_scale(splits[9], (N, E), ((1, 4),), -0.2, 0.2), -3.9, -0.7)
    d_skip = jnp.clip(0.5 + 1.0 * jax.random.uniform(splits[10], (E,), jnp.float32) ** block_scale(splits[10], (E,), ((0, 4),), -0.2, 0.2), 0.5, 1.5)
    w_out = bell_draw(splits[11], (E, D), E ** -0.5, 0.125, ((0, 4),))
    mlp_gain = jnp.clip(1.0 + 0.1 * jax.random.normal(splits[12], (D,), jnp.float32), 0.5, 1.5)
    w_gate = bell_draw(splits[13], (D, FF), D ** -0.5, 0.125, ((1, 4),))
    w_up = bell_draw(splits[14], (D, FF), D ** -0.5, 0.125, ((1, 4),))
    w_down = bell_draw(splits[15], (FF, D), FF ** -0.5, 0.09375, ((0, 4),))
    prompt_lengths = draw_prompt_lengths(jax.random.fold_in(splits[18], 71), 0)
    request_prompt = draw_request_prompt(jax.random.fold_in(splits[18], 71), 0)
    return {"tokens": tokens, "norm_gain": norm_gain, "w_x": w_x, "w_z": w_z, "conv_w": conv_w, "conv_b": conv_b, "w_xproj": w_xproj, "w_dt": w_dt, "dt_bias": dt_bias, "a_log": a_log, "d_skip": d_skip, "w_out": w_out, "mlp_gain": mlp_gain, "w_gate": w_gate, "w_up": w_up, "w_down": w_down, "prompt_lengths": prompt_lengths, "request_prompt": request_prompt}


EPSILON = 1e-05

def rms_norm(values, gain):
    scale = lax.rsqrt(lax.optimization_barrier(jnp.mean(values * values, axis=-1, keepdims=True)) + EPSILON)
    return values * scale * gain.astype(jnp.float32)

def grouped_product(left, right, groups):
    group_width = left.shape[1] // groups
    running_sum = jnp.zeros((left.shape[0], right.shape[1]), jnp.float32)
    for group_index in range(groups):
        lower = group_index * group_width
        upper = lower + group_width
        part_value = jnp.dot(left[:, lower:upper], right[lower:upper], preferred_element_type=jnp.float32).astype(jnp.bfloat16)
        part_value = lax.optimization_barrier(part_value)
        running_sum = running_sum + part_value.astype(jnp.float32)
    return running_sum

def reference(tokens, norm_gain, w_x, w_z, conv_w, conv_b, w_xproj, w_dt, dt_bias, a_log, d_skip, w_out, mlp_gain, w_gate, w_up, w_down, prompt_lengths, request_prompt):
    places = jnp.arange(TOKENS, dtype=jnp.int32)
    prompt_end = jnp.cumsum(prompt_lengths).astype(jnp.int32)
    prompt_start = (prompt_end - prompt_lengths).astype(jnp.int32)
    prompt_ids = jnp.arange(PROMPTS, dtype=jnp.int32)
    prompt_of = lax.optimization_barrier(jnp.sum((places[:, None] >= prompt_end[None, :]).astype(jnp.int32), axis=1))
    start_of = lax.optimization_barrier(jnp.sum(jnp.where(prompt_of[:, None] == prompt_ids[None, :], prompt_start[None, :], 0), axis=1)).astype(jnp.int32)
    offset = places - start_of
    starts_here = jnp.any(places[:, None] == prompt_start[None, :], axis=1)
    ends_here = jnp.any(places[:, None] == prompt_end[None, :] - 1, axis=1)
    is_live = prompt_of < PROMPTS
    normed = rms_norm(tokens.astype(jnp.float32), norm_gain).astype(jnp.bfloat16)
    x_branch = jnp.dot(normed, w_x, preferred_element_type=jnp.float32).astype(jnp.bfloat16)
    z_branch = jnp.dot(normed, w_z, preferred_element_type=jnp.float32).astype(jnp.bfloat16)
    edge_len = K - 1
    padded = jnp.concatenate([jnp.zeros((edge_len, E), jnp.bfloat16), x_branch], axis=0)
    conv_sum = jnp.zeros((TOKENS, E), jnp.float32) + conv_b.astype(jnp.float32)[None, :]
    for lag_steps in range(K):
        window = padded[edge_len - lag_steps:edge_len - lag_steps + TOKENS].astype(jnp.float32)
        reach_mask = (offset >= lag_steps).astype(jnp.float32)[:, None]
        conv_sum = conv_sum + conv_w[edge_len - lag_steps].astype(jnp.float32)[None, :] * window * reach_mask
    conv_out = jax.nn.silu(conv_sum).astype(jnp.bfloat16)
    projected = jnp.dot(conv_out, w_xproj, preferred_element_type=jnp.float32)
    low_rank = projected[:, :R].astype(jnp.bfloat16)
    in_map = projected[:, R:R + N]
    out_map = projected[:, R + N:]
    step_size = jax.nn.softplus(jnp.dot(low_rank, w_dt, preferred_element_type=jnp.float32) + dt_bias.astype(jnp.float32)[None, :])
    decay_rates = -jnp.exp(a_log.astype(jnp.float32))
    driven = step_size * conv_out.astype(jnp.float32)
    carry_on = 1.0 - starts_here.astype(jnp.float32)
    slot_of = jnp.minimum(prompt_of, PROMPTS - 1).astype(jnp.int32)

    def advance(carry, inputs):
        state, finals = carry
        step_now, driven_now, in_now, out_now, keep_now, end_now, slot_now = inputs
        state = jnp.exp(step_now[None, :] * decay_rates) * keep_now * state + driven_now[None, :] * in_now[:, None]
        finals = finals.at[slot_now].add(state * end_now)
        return ((state, finals), lax.optimization_barrier(jnp.sum(out_now[:, None] * state, axis=0)))
    start_carry = (jnp.zeros((N, E), jnp.float32), jnp.zeros((PROMPTS, N, E), jnp.float32))
    scanned = (step_size, driven, in_map, out_map, carry_on, ends_here.astype(jnp.float32), slot_of)
    (last_state, finals), mixer_y = lax.scan(advance, start_carry, scanned)
    mixer_y = mixer_y + d_skip.astype(jnp.float32)[None, :] * conv_out.astype(jnp.float32)
    gated = (mixer_y * jax.nn.silu(z_branch.astype(jnp.float32))).astype(jnp.bfloat16)
    residual = tokens.astype(jnp.float32) + grouped_product(gated, w_out, N_TP)
    normed_two = rms_norm(residual, mlp_gain).astype(jnp.bfloat16)
    gate_val = jnp.dot(normed_two, w_gate, preferred_element_type=jnp.float32)
    up_val = jnp.dot(normed_two, w_up, preferred_element_type=jnp.float32)
    hidden = (jax.nn.silu(gate_val) * up_val).astype(jnp.bfloat16)
    summed = residual + grouped_product(hidden, w_down, N_TP)
    mixed_out = (summed * is_live.astype(jnp.float32)[:, None]).astype(jnp.bfloat16)
    lag_ids = jnp.arange(edge_len, dtype=jnp.int32)
    target = prompt_end[:, None] - edge_len + lag_ids[None, :]
    inside = target >= prompt_start[:, None]
    edge_rows = jnp.where(inside[:, :, None], x_branch[jnp.maximum(target, 0)], jnp.zeros((), jnp.bfloat16))
    req_states = finals[request_prompt]
    req_edges = edge_rows[request_prompt]
    return (mixed_out, req_states, req_edges)
```

```python
import jax
import jax.numpy as jnp
from jax import lax
from jax.experimental import pallas as pl
from jax.experimental.pallas import tpu as pltpu
from jax.sharding import PartitionSpec as P

EPSILON = 1e-05
F32 = jnp.float32
BF16 = jnp.bfloat16
FAR = 1e30
GROUP = 8


def rms_norm(values, gain):
    scale = lax.rsqrt(jnp.mean(values * values, axis=-1, keepdims=True) + EPSILON)
    return values * scale * gain


def silu(v):
    return v * jax.nn.sigmoid(v)


def dot(a, b):
    return jnp.dot(a, b, preferred_element_type=F32)


def remote(src, dst, send_sem, recv_sem, device):
    return pltpu.make_async_remote_copy(
        src_ref=src,
        dst_ref=dst,
        send_sem=send_sem,
        recv_sem=recv_sem,
        device_id=device,
        device_id_type=pl.DeviceIdType.MESH,
    )


NAMES = (
    "tokens", "norm_gain", "w_x", "w_z", "conv_w", "conv_b", "w_xproj", "w_dt", "dt_bias",
    "a_log", "d_skip", "w_out", "mlp_gain", "w_gate", "w_up", "w_down",
)
EARLY = NAMES[:3]
LATE = ("w_out", "w_gate", "w_up", "w_down")
NEXT = tuple(k for k in NAMES if k not in EARLY + LATE)


def make_local(S, T):
    X = T // 2

    def local(*args):
        arrays = dict(zip(NAMES, args[:16]))
        prompt_lengths, request_prompt = args[16:]
        for k in ("norm_gain", "conv_b", "dt_bias", "d_skip", "mlp_gain"):
            arrays[k] = arrays[k][None, :]
        B, D = arrays["tokens"].shape
        E = arrays["w_x"].shape[1]
        K = arrays["conv_w"].shape[0]
        R = arrays["w_dt"].shape[0]
        N = arrays["a_log"].shape[0]
        M = arrays["w_xproj"].shape[1]
        FF = arrays["w_gate"].shape[1]
        NP = prompt_lengths.shape[0]
        NR = request_prompt.shape[0]
        rc = B // T
        J = K - 1
        EP = -(-NP * J // 16) * 16
        FR = NP * N + EP
        groups = B // GROUP

        scratch = {k: pltpu.VMEM(arrays[k].shape, arrays[k].dtype) for k in NAMES}
        scratch.update(
            load_sem=pltpu.SemaphoreType.DMA((16,)),
            edge_s=pltpu.VMEM((16, E), BF16),
            edge_r=pltpu.VMEM((16, E), BF16),
            edge_sem=pltpu.SemaphoreType.DMA((2,)),
            ext=pltpu.VMEM((8 + B, E), F32),
            z=pltpu.VMEM((B, E), F32),
            pj=pltpu.VMEM((T, B, M), BF16),
            pj_send=pltpu.SemaphoreType.DMA((T,)),
            pj_recv=pltpu.SemaphoreType.DMA((T,)),
            mp=pltpu.VMEM((B, 256), F32),
            m3=pltpu.VMEM((groups, 2 * N, GROUP), F32),
            stepd=pltpu.VMEM((B, E), F32),
            drv=pltpu.VMEM((B, E), F32),
            dec=pltpu.VMEM((B, N, E), F32),
            sts=pltpu.VMEM((B, N, E), F32),
            y=pltpu.VMEM((B, E), F32),
            ssum=pltpu.VMEM((S, 1, E), F32),
            sbuf=pltpu.VMEM((S, N, E), BF16),
            a_send=pltpu.SemaphoreType.DMA((S,)),
            a_recv=pltpu.SemaphoreType.DMA((S,)),
            b_send=pltpu.SemaphoreType.DMA((S,)),
            b_recv=pltpu.SemaphoreType.DMA((S,)),
            fin=pltpu.VMEM((S, FR, E), BF16),
            f_send=pltpu.SemaphoreType.DMA((S,)),
            f_recv=pltpu.SemaphoreType.DMA((S,)),
            stat=pltpu.VMEM((NP, N, E), F32),
            edg=pltpu.VMEM((NP, 8, E), F32),
            part=pltpu.VMEM((2, X, rc, D), BF16),
            recv1=pltpu.VMEM((X, rc, D), BF16),
            psb=pltpu.VMEM((X, rc, D), BF16),
            recv2=pltpu.VMEM((X, X, rc, D), BF16),
            res=pltpu.VMEM((X, rc, D), F32),
            n2=pltpu.VMEM((2, X, rc, D), BF16),
            hid=pltpu.VMEM((B, FF), BF16),
            partb=pltpu.VMEM((2, X, rc, D), BF16),
            recv3=pltpu.VMEM((X, rc, D), BF16),
            psb2=pltpu.VMEM((X, rc, D), BF16),
            recv4=pltpu.VMEM((X, rc, D), BF16),
            c_send=pltpu.SemaphoreType.DMA((3,)),
            c_recv=pltpu.SemaphoreType.DMA((3,)),
            x_send=pltpu.SemaphoreType.DMA((2, X)),
            x_recv=pltpu.SemaphoreType.DMA((2, X)),
        )
        keys = list(scratch)

        def kernel(*refs):
            hbm = dict(zip(NAMES, refs[:16]))
            lens, reqs, out, out_states, out_edges = refs[16:21]
            s = dict(zip(keys, refs[21:]))
            seq = lax.axis_index("seq")
            tp = lax.axis_index("tp")
            x = lax.div(tp, 2)
            c = lax.rem(tp, 2)
            sib = {"tp": x * 2 + 1 - c}

            loads = {
                k: pltpu.make_async_copy(hbm[k], s[k], s["load_sem"].at[i])
                for i, k in enumerate(NAMES)
            }
            for k in EARLY:
                loads[k].start()

            barrier = pltpu.get_barrier_semaphore()
            for i in range(1, T):
                pl.semaphore_signal(
                    barrier, 1, device_id={"tp": lax.rem(tp + i, T)},
                    device_id_type=pl.DeviceIdType.MESH,
                )

            @pl.loop(1, S)
            def _(i):
                pl.semaphore_signal(
                    barrier, 1, device_id={"seq": lax.rem(seq + i, S)},
                    device_id_type=pl.DeviceIdType.MESH,
                )

            for k in NEXT:
                loads[k].start()

            ends, starts = [], []
            total = jnp.int32(0)
            for p in range(NP):
                starts.append(total)
                total = total + lens[p]
                ends.append(total)
            first = seq * B
            places = first + lax.broadcasted_iota(jnp.int32, (B, 1), 0)
            start_of = jnp.zeros((B, 1), jnp.int32)
            begins = jnp.zeros((B, 1), jnp.int32)
            for p in range(NP):
                here = (places >= starts[p]) & (places < ends[p])
                start_of = jnp.where(here, starts[p], start_of)
                begins = jnp.where(places == starts[p], 1, begins)
            offset = places - start_of

            loads["tokens"].wait()
            loads["norm_gain"].wait()
            normed = rms_norm(s["tokens"][...].astype(F32), s["norm_gain"][...]).astype(BF16)
            loads["w_x"].wait()
            for k in LATE:
                loads[k].start()
            xb = dot(normed, s["w_x"][...]).astype(BF16)
            s["edge_s"][...] = xb[B - 16 :]
            xf = xb.astype(F32)
            s["ext"][8:, :] = xf
            pl.semaphore_wait(barrier, T - 1 + S - 1)
            edge = remote(
                s["edge_s"], s["edge_r"], s["edge_sem"].at[0], s["edge_sem"].at[1],
                {"seq": lax.rem(seq + 1, S)},
            )

            @pl.when(seq < S - 1)
            def _():
                edge.start()

            for k in NEXT:
                loads[k].wait()
            half = E // 2
            s["z"][:, :half] = dot(normed, s["w_z"][:, :half])

            @pl.when(seq > 0)
            def _():
                edge.wait_recv()
                s["ext"][0:8, :] = s["edge_r"][...].astype(F32)[8:]

            @pl.when(seq == 0)
            def _():
                s["ext"][0:8, :] = jnp.zeros((8, E), F32)

            acc = jnp.zeros((B, E), F32) + s["conv_b"][...]
            for lag in range(K):
                window = s["ext"][8 - lag : 8 - lag + B, :]
                mask = jnp.where(offset >= lag, 1.0, 0.0)
                acc = acc + s["conv_w"][J - lag : J - lag + 1, :] * window * mask
            conv_out = silu(acc).astype(BF16)

            s["pj"][0] = dot(conv_out, s["w_xproj"][...]).astype(BF16)
            pj = []
            for i in range(1, T):
                pj.append(
                    remote(
                        s["pj"].at[0], s["pj"].at[i], s["pj_send"].at[i], s["pj_recv"].at[i],
                        {"tp": lax.rem(tp + i, T)},
                    )
                )
                pj[-1].start()
            s["z"][:, half:] = dot(normed, s["w_z"][:, half:])
            rates = -jnp.exp(s["a_log"][...])
            conv = conv_out.astype(F32)
            s["mp"][...] = jnp.zeros((B, 256), F32)
            projected = s["pj"][0].astype(F32)
            for i in range(1, T):
                pj[i - 1].wait_recv()
                projected = projected + s["pj"][i].astype(F32)
            s["mp"][:, :M] = projected
            maps = jnp.transpose(s["mp"][:, R : R + 128])
            for g in range(groups):
                s["m3"][g] = maps[: 2 * N, g * GROUP : (g + 1) * GROUP]
            low = s["mp"][:, :R].astype(BF16)
            pre = dot(low, s["w_dt"][...]) + s["dt_bias"][...]
            step = jnp.maximum(pre, 0.0) + jnp.log1p(jnp.exp(-jnp.abs(pre)))
            s["drv"][...] = step * conv
            stepd = jnp.where(begins > 0, FAR, step)
            s["stepd"][...] = stepd
            s["ssum"][seq] = jnp.sum(stepd, axis=0, keepdims=True)

            def send_a(d):
                return remote(
                    s["ssum"].at[seq], s["ssum"].at[seq], s["a_send"].at[d],
                    s["a_recv"].at[seq], {"seq": d},
                )

            def send_b(d):
                return remote(
                    s["sbuf"].at[seq], s["sbuf"].at[seq], s["b_send"].at[d],
                    s["b_recv"].at[seq], {"seq": d},
                )

            @pl.loop(seq + 1, S)
            def _(d):
                send_a(d).start()

            def one(g, st):
                base = pl.multiple_of(g * GROUP, GROUP)
                sg = s["stepd"][pl.ds(base, GROUP), :]
                dg = s["drv"][pl.ds(base, GROUP), :]
                mg = s["m3"][g]
                for i in range(GROUP):
                    decay = jnp.exp(sg[i : i + 1, :] * rates)
                    s["dec"][base + i] = decay
                    st = decay * st + dg[i : i + 1, :] * mg[:N, i : i + 1]
                return st

            last = lax.fori_loop(0, groups, one, jnp.zeros((N, E), F32))
            s["sbuf"][seq] = last.astype(BF16)

            @pl.loop(seq + 1, S)
            def _(d):
                send_b(d).start()

            s["z"][...] = silu(s["z"][...].astype(BF16).astype(F32))

            def join(e, st):
                remote(
                    s["ssum"].at[e], s["ssum"].at[e], s["a_send"].at[e], s["a_recv"].at[e],
                    {"seq": e},
                ).wait_recv()
                remote(
                    s["sbuf"].at[e], s["sbuf"].at[e], s["b_send"].at[e], s["b_recv"].at[e],
                    {"seq": e},
                ).wait_recv()
                return jnp.exp(s["ssum"][e] * rates) * st + s["sbuf"][e].astype(F32)

            state_in = lax.fori_loop(0, seq, join, jnp.zeros((N, E), F32))

            def two(g, st):
                base = pl.multiple_of(g * GROUP, GROUP)
                dg = s["drv"][pl.ds(base, GROUP), :]
                mg = s["m3"][g]
                rows = []
                for i in range(GROUP):
                    st = s["dec"][base + i] * st + dg[i : i + 1, :] * mg[:N, i : i + 1]
                    s["sts"][base + i] = st
                    rows.append(jnp.sum(st * mg[N:, i : i + 1], axis=0, keepdims=True))
                s["y"][pl.ds(base, GROUP), :] = jnp.concatenate(rows, axis=0)
                return st

            lax.fori_loop(0, groups, two, state_in)
            gated = ((s["y"][...] + s["d_skip"][...] * conv) * s["z"][...]).astype(BF16)

            loads["w_out"].wait()
            cols = min(D, 512)

            def project_out(left, w, dest, permuted):
                @pl.loop(0, D // cols)
                def _(j):
                    at = pl.ds(pl.multiple_of(j * cols, cols), cols)
                    val = dot(left(), w[:, at]).astype(BF16)
                    for q in range(T):
                        rows = val[q * rc : (q + 1) * rc]
                        if permuted:
                            dest[q // X, q % X, :, at] = rows
                        else:
                            dest[q % 2, q // 2, :, at] = rows

            s["hid"][:, :E] = gated
            project_out(lambda: s["hid"][:, :E], s["w_out"], s["part"], False)
            first_sum = remote(
                s["part"].at[1 - c], s["recv1"], s["c_send"].at[0], s["c_recv"].at[0], sib
            )
            first_sum.start()

            for p in range(NP):
                row = jnp.clip(ends[p] - 1 - first, 0, B - 1)
                s["fin"][seq, p * N : (p + 1) * N, :] = s["sts"][row].astype(BF16)
            rows = []
            for p in range(NP):
                for j in range(J):
                    target = jnp.clip(ends[p] - J + j - first + 8, 0, B + 7)
                    got = s["ext"][pl.ds(target, 1), :]
                    rows.append(jnp.where(ends[p] - J + j >= starts[p], got, 0.0))
            rows += [jnp.zeros((1, E), F32)] * (EP - NP * J)
            s["fin"][seq, NP * N :, :] = jnp.concatenate(rows, axis=0).astype(BF16)

            def send_f(i):
                return remote(
                    s["fin"].at[seq], s["fin"].at[seq], s["f_send"].at[i], s["f_recv"].at[seq],
                    {"seq": lax.rem(seq + i, S)},
                )

            @pl.loop(1, S)
            def _(i):
                send_f(i).start()

            first_sum.wait_recv()
            s["psb"][...] = (s["part"][c].astype(F32) + s["recv1"][...].astype(F32)).astype(BF16)
            over_x = []
            for i in range(1, X):
                over_x.append(
                    remote(
                        s["psb"], s["recv2"].at[i], s["x_send"].at[0, i], s["x_recv"].at[0, i],
                        {"tp": lax.rem(x + i, X) * 2 + c},
                    )
                )
                over_x[-1].start()
            for r in over_x:
                r.wait_recv()
            for b in range(X):
                at = pl.ds(pl.multiple_of((2 * b + c) * rc, rc), rc)
                val = s["tokens"][at, :].astype(F32) + s["psb"][b].astype(F32)
                for i in range(1, X):
                    val = val + s["recv2"][i, b].astype(F32)
                s["res"][b] = val
                s["n2"][c, b] = rms_norm(val, s["mlp_gain"][...]).astype(BF16)
            swap = remote(
                s["n2"].at[c], s["n2"].at[c], s["c_send"].at[1], s["c_recv"].at[1], sib
            )
            swap.start()
            for k in ("w_gate", "w_up", "w_down"):
                loads[k].wait()
            swap.wait_recv()

            wide = min(FF, 256)

            @pl.loop(0, FF // wide)
            def _(j):
                at = pl.ds(pl.multiple_of(j * wide, wide), wide)
                left = s["n2"][...].reshape(B, D)
                gate = dot(left, s["w_gate"][:, at])
                up = dot(left, s["w_up"][:, at])
                s["hid"][:, at] = (silu(gate) * up).astype(BF16)

            project_out(lambda: s["hid"][...], s["w_down"], s["partb"], True)
            second_sum = remote(
                s["partb"].at[1 - c], s["recv3"], s["c_send"].at[2], s["c_recv"].at[2], sib
            )
            second_sum.start()
            second_sum.wait_recv()
            s["psb2"][...] = (s["partb"][c].astype(F32) + s["recv3"][...].astype(F32)).astype(BF16)
            back = []
            for i in range(1, X):
                there = lax.rem(x + i, X)
                back.append(
                    remote(
                        s["psb2"].at[there], s["recv4"].at[i], s["x_send"].at[1, i],
                        s["x_recv"].at[1, i], {"tp": there * 2 + c},
                    )
                )
                back[-1].start()

            @pl.loop(1, S)
            def _(i):
                e = lax.rem(seq + i, S)
                remote(
                    s["fin"].at[e], s["fin"].at[e], s["f_send"].at[i], s["f_recv"].at[e],
                    {"seq": e},
                ).wait_recv()

            for p in range(NP):
                owner = lax.div(ends[p] - 1, B)
                got = s["fin"][owner]
                s["stat"][p] = got[p * N : (p + 1) * N].astype(F32)
                s["edg"][p, 0:J, :] = got[NP * N :].astype(F32)[p * J : (p + 1) * J]
            for r in range(NR):
                out_states[r] = s["stat"][reqs[r]]
                out_edges[r] = s["edg"][reqs[r], 0:J, :]

            val = s["res"][x] + s["psb2"][x].astype(F32)
            for i in range(1, X):
                back[i - 1].wait_recv()
                val = val + s["recv4"][i].astype(F32)
            slot = first + tp * rc + lax.broadcasted_iota(jnp.int32, (rc, 1), 0)
            out[...] = (val * jnp.where(slot < total, 1.0, 0.0)).astype(BF16)

            @pl.when(seq < S - 1)
            def _():
                edge.wait_send()

            for r in pj + over_x + back + [first_sum, swap, second_sum]:
                r.wait_send()

            @pl.loop(seq + 1, S)
            def _(d):
                send_a(d).wait_send()
                send_b(d).wait_send()

            @pl.loop(1, S)
            def _(i):
                send_f(i).wait_send()

        anyspec = pl.BlockSpec(memory_space=pl.ANY)
        smem = pl.BlockSpec(memory_space=pltpu.SMEM)
        vmem = pl.BlockSpec(memory_space=pltpu.VMEM)
        mixed_out, req_states, req_edges = pl.pallas_call(
            kernel,
            out_shape=(
                jax.ShapeDtypeStruct((rc, D), BF16),
                jax.ShapeDtypeStruct((NR, N, E), F32),
                jax.ShapeDtypeStruct((NR, J, E), F32),
            ),
            in_specs=[anyspec] * 16 + [smem] * 2,
            out_specs=(vmem,) * 3,
            scratch_shapes=list(scratch.values()),
            compiler_params=pltpu.CompilerParams(
                collective_id=0, has_side_effects=True, vmem_limit_bytes=58 * 2**20
            ),
        )(*[arrays[k] for k in NAMES], prompt_lengths, request_prompt)
        return mixed_out, req_states, req_edges.astype(BF16)

    return local


def solution(mesh):
    placed = (
        P("seq", None),
        P(),
        P(None, "tp"),
        P(None, "tp"),
        P(None, "tp"),
        P("tp"),
        P("tp", None),
        P(None, "tp"),
        P("tp"),
        P(None, "tp"),
        P("tp"),
        P("tp", None),
        P(),
        P(None, "tp"),
        P(None, "tp"),
        P("tp", None),
        P(),
        P("seq"),
    )
    return jax.shard_map(
        make_local(mesh.shape["seq"], mesh.shape["tp"]),
        mesh=mesh,
        in_specs=placed,
        out_specs=(P(("seq", "tp"), None), P("seq", None, "tp"), P("seq", None, "tp")),
        check_vma=False,
    )
```

```python
import jax
import jax.numpy as jnp
from jax import lax
from jax.experimental import pallas as pl
from jax.experimental.pallas import tpu as pltpu
from jax.sharding import PartitionSpec as P

EPSILON = 1e-05
F32 = jnp.float32
BF16 = jnp.bfloat16
FAR = 1e30
GROUP = 8


def rms_norm(values, gain):
    scale = lax.rsqrt(jnp.mean(values * values, axis=-1, keepdims=True) + EPSILON)
    return values * scale * gain


def silu(v):
    return v * jax.nn.sigmoid(v)


def dot(a, b):
    return jnp.dot(a, b, preferred_element_type=F32)


def remote(src, dst, send_sem, recv_sem, device):
    return pltpu.make_async_remote_copy(
        src_ref=src,
        dst_ref=dst,
        send_sem=send_sem,
        recv_sem=recv_sem,
        device_id=device,
        device_id_type=pl.DeviceIdType.MESH,
    )


NAMES = (
    "tokens", "norm_gain", "w_x", "w_z", "conv_w", "conv_b", "w_xproj", "w_dt", "dt_bias",
    "a_log", "d_skip", "w_out", "mlp_gain", "w_gate", "w_up", "w_down",
)
EARLY = NAMES[:3]
LATE = ("w_out", "w_gate", "w_up", "w_down")
NEXT = tuple(k for k in NAMES if k not in EARLY + LATE)


def make_local(S, T):
    X = T // 2

    def local(*args):
        arrays = dict(zip(NAMES, args[:16]))
        prompt_lengths, request_prompt = args[16:]
        for k in ("norm_gain", "conv_b", "dt_bias", "d_skip", "mlp_gain"):
            arrays[k] = arrays[k][None, :]
        B, D = arrays["tokens"].shape
        E = arrays["w_x"].shape[1]
        K = arrays["conv_w"].shape[0]
        R = arrays["w_dt"].shape[0]
        N = arrays["a_log"].shape[0]
        M = arrays["w_xproj"].shape[1]
        arrays["w_xproj"] = arrays["w_xproj"].T
        FF = arrays["w_gate"].shape[1]
        NP = prompt_lengths.shape[0]
        NR = request_prompt.shape[0]
        rc = B // T
        J = K - 1
        EP = -(-NP * J // 16) * 16
        FR = NP * N + EP
        groups = B // GROUP
        cw = min(D, 512)
        CH = D // cw

        scratch = {k: pltpu.VMEM(arrays[k].shape, arrays[k].dtype) for k in NAMES}
        scratch.update(
            load_sem=pltpu.SemaphoreType.DMA((16,)),
            edge_s=pltpu.VMEM((16, E), BF16),
            edge_r=pltpu.VMEM((16, E), BF16),
            edge_sem=pltpu.SemaphoreType.DMA((2,)),
            ext=pltpu.VMEM((8 + B, E), F32),
            z=pltpu.VMEM((B, E), F32),
            pj=pltpu.VMEM((T, B, M), BF16),
            pj_send=pltpu.SemaphoreType.DMA((T,)),
            pj_recv=pltpu.SemaphoreType.DMA((T,)),
            mp=pltpu.VMEM((B, 256), F32),
            m3=pltpu.VMEM((groups, 2 * N, GROUP), F32),
            stepd=pltpu.VMEM((B, E), F32),
            drv=pltpu.VMEM((B, E), F32),
            dec=pltpu.VMEM((B, N, E), F32),
            sts=pltpu.VMEM((B, N, E), F32),
            y=pltpu.VMEM((B, E), F32),
            ssum=pltpu.VMEM((S, 1, E), F32),
            sbuf=pltpu.VMEM((S, N, E), BF16),
            a_send=pltpu.SemaphoreType.DMA((S,)),
            a_recv=pltpu.SemaphoreType.DMA((S,)),
            b_send=pltpu.SemaphoreType.DMA((S,)),
            b_recv=pltpu.SemaphoreType.DMA((S,)),
            fin=pltpu.VMEM((S, FR, E), BF16),
            f_send=pltpu.SemaphoreType.DMA((S,)),
            f_recv=pltpu.SemaphoreType.DMA((S,)),
            stat=pltpu.VMEM((NP, N, E), F32),
            edg=pltpu.VMEM((NP, 8, E), F32),
            part=pltpu.VMEM((CH, 2, X, rc, cw), BF16),
            recv1=pltpu.VMEM((CH, X, rc, cw), BF16),
            psb=pltpu.VMEM((CH, X, rc, cw), BF16),
            recv2=pltpu.VMEM((X, CH, X, rc, cw), BF16),
            res=pltpu.VMEM((X, rc, D), F32),
            n2=pltpu.VMEM((2, X, rc, D), BF16),
            hid=pltpu.VMEM((B, FF), BF16),
            partb=pltpu.VMEM((CH, 2, X, rc, cw), BF16),
            recv3=pltpu.VMEM((CH, X, rc, cw), BF16),
            psb2=pltpu.VMEM((CH, X, rc, cw), BF16),
            recv4=pltpu.VMEM((X, CH, rc, cw), BF16),
            swap_sem=pltpu.SemaphoreType.DMA((2,)),
            c_send=pltpu.SemaphoreType.DMA((2, CH)),
            c_recv=pltpu.SemaphoreType.DMA((2, CH)),
            x_send=pltpu.SemaphoreType.DMA((2, CH, X)),
            x_recv=pltpu.SemaphoreType.DMA((2, CH, X)),
        )
        keys = list(scratch)

        def kernel(*refs):
            hbm = dict(zip(NAMES, refs[:16]))
            lens, reqs, out, out_states, out_edges = refs[16:21]
            s = dict(zip(keys, refs[21:]))
            seq = lax.axis_index("seq")
            tp = lax.axis_index("tp")
            x = lax.div(tp, 2)
            c = lax.rem(tp, 2)
            sib = {"tp": x * 2 + 1 - c}

            loads = {
                k: pltpu.make_async_copy(hbm[k], s[k], s["load_sem"].at[i])
                for i, k in enumerate(NAMES)
            }
            for k in EARLY:
                loads[k].start()

            barrier = pltpu.get_barrier_semaphore()
            for i in range(1, T):
                pl.semaphore_signal(
                    barrier, 1, device_id={"tp": lax.rem(tp + i, T)},
                    device_id_type=pl.DeviceIdType.MESH,
                )

            @pl.loop(1, S)
            def _(i):
                pl.semaphore_signal(
                    barrier, 1, device_id={"seq": lax.rem(seq + i, S)},
                    device_id_type=pl.DeviceIdType.MESH,
                )

            for k in NEXT:
                loads[k].start()

            ends, starts = [], []
            total = jnp.int32(0)
            for p in range(NP):
                starts.append(total)
                total = total + lens[p]
                ends.append(total)
            first = seq * B
            places = first + lax.broadcasted_iota(jnp.int32, (B, 1), 0)
            start_of = jnp.zeros((B, 1), jnp.int32)
            begins = jnp.zeros((B, 1), jnp.int32)
            for p in range(NP):
                here = (places >= starts[p]) & (places < ends[p])
                start_of = jnp.where(here, starts[p], start_of)
                begins = jnp.where(places == starts[p], 1, begins)
            offset = places - start_of

            loads["tokens"].wait()
            loads["norm_gain"].wait()
            normed = rms_norm(s["tokens"][...].astype(F32), s["norm_gain"][...]).astype(BF16)
            loads["w_x"].wait()
            for k in LATE:
                loads[k].start()
            xb = dot(normed, s["w_x"][...]).astype(BF16)
            s["edge_s"][...] = xb[B - 16 :]
            xf = xb.astype(F32)
            s["ext"][8:, :] = xf
            pl.semaphore_wait(barrier, T - 1 + S - 1)
            edge = remote(
                s["edge_s"], s["edge_r"], s["edge_sem"].at[0], s["edge_sem"].at[1],
                {"seq": lax.rem(seq + 1, S)},
            )

            @pl.when(seq < S - 1)
            def _():
                edge.start()

            for k in NEXT:
                loads[k].wait()
            half = E // 2
            s["z"][:, :half] = dot(normed, s["w_z"][:, :half])

            @pl.when(seq > 0)
            def _():
                edge.wait_recv()
                s["ext"][0:8, :] = s["edge_r"][...].astype(F32)[8:]

            @pl.when(seq == 0)
            def _():
                s["ext"][0:8, :] = jnp.zeros((8, E), F32)

            acc = jnp.zeros((B, E), F32) + s["conv_b"][...]
            for lag in range(K):
                window = s["ext"][8 - lag : 8 - lag + B, :]
                mask = jnp.where(offset >= lag, 1.0, 0.0)
                acc = acc + s["conv_w"][J - lag : J - lag + 1, :] * window * mask
            conv_out = silu(acc).astype(BF16)

            s["pj"][0] = lax.dot_general(
                conv_out, s["w_xproj"][...], (((1,), (1,)), ((), ())),
                preferred_element_type=F32,
            ).astype(BF16)
            pj = []
            for i in range(1, T):
                pj.append(
                    remote(
                        s["pj"].at[0], s["pj"].at[i], s["pj_send"].at[i], s["pj_recv"].at[i],
                        {"tp": lax.rem(tp + i, T)},
                    )
                )
                pj[-1].start()
            s["z"][:, half:] = dot(normed, s["w_z"][:, half:])
            rates = -jnp.exp(s["a_log"][...])
            conv = conv_out.astype(F32)
            s["mp"][...] = jnp.zeros((B, 256), F32)
            projected = s["pj"][0].astype(F32)
            for i in range(1, T):
                pj[i - 1].wait_recv()
                projected = projected + s["pj"][i].astype(F32)
            s["mp"][:, :M] = projected
            maps = jnp.transpose(s["mp"][:, R : R + 128])
            for g in range(groups):
                s["m3"][g] = maps[: 2 * N, g * GROUP : (g + 1) * GROUP]
            low = s["mp"][:, :R].astype(BF16)
            pre = dot(low, s["w_dt"][...]) + s["dt_bias"][...]
            step = jnp.maximum(pre, 0.0) + jnp.log1p(jnp.exp(-jnp.abs(pre)))
            s["drv"][...] = step * conv
            stepd = jnp.where(begins > 0, FAR, step)
            s["stepd"][...] = stepd
            s["ssum"][seq] = jnp.sum(stepd, axis=0, keepdims=True)

            def send_a(d):
                return remote(
                    s["ssum"].at[seq], s["ssum"].at[seq], s["a_send"].at[d],
                    s["a_recv"].at[seq], {"seq": d},
                )

            def send_b(d):
                return remote(
                    s["sbuf"].at[seq], s["sbuf"].at[seq], s["b_send"].at[d],
                    s["b_recv"].at[seq], {"seq": d},
                )

            @pl.loop(seq + 1, S)
            def _(d):
                send_a(d).start()

            def one(g, st):
                base = pl.multiple_of(g * GROUP, GROUP)
                sg = s["stepd"][pl.ds(base, GROUP), :]
                dg = s["drv"][pl.ds(base, GROUP), :]
                mg = s["m3"][g]
                for i in range(GROUP):
                    decay = jnp.exp(sg[i : i + 1, :] * rates)
                    s["dec"][base + i] = decay
                    st = decay * st + dg[i : i + 1, :] * mg[:N, i : i + 1]
                return st

            last = lax.fori_loop(0, groups, one, jnp.zeros((N, E), F32))
            s["sbuf"][seq] = last.astype(BF16)

            @pl.loop(seq + 1, S)
            def _(d):
                send_b(d).start()

            s["z"][...] = silu(s["z"][...].astype(BF16).astype(F32))

            def join(e, st):
                remote(
                    s["ssum"].at[e], s["ssum"].at[e], s["a_send"].at[e], s["a_recv"].at[e],
                    {"seq": e},
                ).wait_recv()
                remote(
                    s["sbuf"].at[e], s["sbuf"].at[e], s["b_send"].at[e], s["b_recv"].at[e],
                    {"seq": e},
                ).wait_recv()
                return jnp.exp(s["ssum"][e] * rates) * st + s["sbuf"][e].astype(F32)

            state_in = lax.fori_loop(0, seq, join, jnp.zeros((N, E), F32))

            def two(g, st):
                base = pl.multiple_of(g * GROUP, GROUP)
                dg = s["drv"][pl.ds(base, GROUP), :]
                mg = s["m3"][g]
                rows = []
                for i in range(GROUP):
                    st = s["dec"][base + i] * st + dg[i : i + 1, :] * mg[:N, i : i + 1]
                    s["sts"][base + i] = st
                    rows.append(jnp.sum(st * mg[N:, i : i + 1], axis=0, keepdims=True))
                s["y"][pl.ds(base, GROUP), :] = jnp.concatenate(rows, axis=0)
                return st

            lax.fori_loop(0, groups, two, state_in)
            gated = ((s["y"][...] + s["d_skip"][...] * conv) * s["z"][...]).astype(BF16)

            loads["w_out"].wait()
            s["hid"][:, :E] = gated
            sums = ([], [])
            over_x = ([], [])

            def chunk(j):
                return slice(j * cw, (j + 1) * cw)

            def in_chip(k, j, left, w, dest, land, place_of):
                val = dot(left, w[:, chunk(j)]).astype(BF16)
                for q in range(T):
                    cc, xx = place_of(q)
                    dest[j, cc, xx] = val[q * rc : (q + 1) * rc]
                r = remote(
                    dest.at[j, 1 - c], land.at[j], s["c_send"].at[k, j], s["c_recv"].at[k, j], sib
                )
                r.start()
                sums[k].append(r)

            def pair_sum(k, j, part, land, dest):
                sums[k][j].wait_recv()
                dest[j] = (part[j, c].astype(F32) + land[j].astype(F32)).astype(BF16)
                for i in range(1, X):
                    there = lax.rem(x + i, X)
                    r = remote(
                        dest.at[j] if k == 0 else dest.at[j, there],
                        s["recv2" if k == 0 else "recv4"].at[i, j],
                        s["x_send"].at[k, j, i],
                        s["x_recv"].at[k, j, i],
                        {"tp": there * 2 + c},
                    )
                    r.start()
                    over_x[k].append(r)

            for j in range(CH + 1):
                if j < CH:
                    in_chip(
                        0, j, s["hid"][:, :E], s["w_out"], s["part"], s["recv1"],
                        lambda q: (q % 2, q // 2),
                    )
                if j > 0:
                    pair_sum(0, j - 1, s["part"], s["recv1"], s["psb"])

            for p in range(NP):
                row = jnp.clip(ends[p] - 1 - first, 0, B - 1)
                s["fin"][seq, p * N : (p + 1) * N, :] = s["sts"][row].astype(BF16)
            rows = []
            for p in range(NP):
                for j in range(J):
                    target = jnp.clip(ends[p] - J + j - first + 8, 0, B + 7)
                    got = s["ext"][pl.ds(target, 1), :]
                    rows.append(jnp.where(ends[p] - J + j >= starts[p], got, 0.0))
            rows += [jnp.zeros((1, E), F32)] * (EP - NP * J)
            s["fin"][seq, NP * N :, :] = jnp.concatenate(rows, axis=0).astype(BF16)

            def send_f(i):
                return remote(
                    s["fin"].at[seq], s["fin"].at[seq], s["f_send"].at[i], s["f_recv"].at[seq],
                    {"seq": lax.rem(seq + i, S)},
                )

            @pl.loop(1, S)
            def _(i):
                send_f(i).start()

            for j in range(CH):
                for i in range(1, X):
                    over_x[0][j * (X - 1) + i - 1].wait_recv()
                for b in range(X):
                    at = pl.ds(pl.multiple_of((2 * b + c) * rc, rc), rc)
                    val = s["tokens"][at, chunk(j)].astype(F32) + s["psb"][j, b].astype(F32)
                    for i in range(1, X):
                        val = val + s["recv2"][i, j, b].astype(F32)
                    s["res"][b, :, chunk(j)] = val
            for b in range(X):
                s["n2"][c, b] = rms_norm(s["res"][b], s["mlp_gain"][...]).astype(BF16)
            swap = remote(
                s["n2"].at[c], s["n2"].at[c], s["swap_sem"].at[0], s["swap_sem"].at[1], sib
            )
            swap.start()
            for k in ("w_gate", "w_up", "w_down"):
                loads[k].wait()
            swap.wait_recv()

            wide = min(FF, 256)

            @pl.loop(0, FF // wide)
            def _(j):
                at = pl.ds(pl.multiple_of(j * wide, wide), wide)
                left = s["n2"][...].reshape(B, D)
                gate = dot(left, s["w_gate"][:, at])
                up = dot(left, s["w_up"][:, at])
                s["hid"][:, at] = (silu(gate) * up).astype(BF16)

            for j in range(CH + 1):
                if j < CH:
                    in_chip(
                        1, j, s["hid"][...], s["w_down"], s["partb"], s["recv3"],
                        lambda q: (q // X, q % X),
                    )
                if j > 0:
                    pair_sum(1, j - 1, s["partb"], s["recv3"], s["psb2"])

            @pl.loop(1, S)
            def _(i):
                e = lax.rem(seq + i, S)
                remote(
                    s["fin"].at[e], s["fin"].at[e], s["f_send"].at[i], s["f_recv"].at[e],
                    {"seq": e},
                ).wait_recv()

            for p in range(NP):
                owner = lax.div(ends[p] - 1, B)
                got = s["fin"][owner]
                s["stat"][p] = got[p * N : (p + 1) * N].astype(F32)
                s["edg"][p, 0:J, :] = got[NP * N :].astype(F32)[p * J : (p + 1) * J]
            for r in range(NR):
                out_states[r] = s["stat"][reqs[r]]
                picked = s["edg"][reqs[r]]
                for j in range(J):
                    out_edges[j, r : r + 1, :] = picked[j : j + 1]

            slot = first + tp * rc + lax.broadcasted_iota(jnp.int32, (rc, 1), 0)
            live = jnp.where(slot < total, 1.0, 0.0)
            for j in range(CH):
                val = s["res"][x, :, chunk(j)] + s["psb2"][j, x].astype(F32)
                for i in range(1, X):
                    over_x[1][j * (X - 1) + i - 1].wait_recv()
                    val = val + s["recv4"][i, j].astype(F32)
                out[:, chunk(j)] = (val * live).astype(BF16)

            @pl.when(seq < S - 1)
            def _():
                edge.wait_send()

            for r in pj + over_x[0] + over_x[1] + sums[0] + sums[1] + [swap]:
                r.wait_send()

            @pl.loop(seq + 1, S)
            def _(d):
                send_a(d).wait_send()
                send_b(d).wait_send()

            @pl.loop(1, S)
            def _(i):
                send_f(i).wait_send()

        anyspec = pl.BlockSpec(memory_space=pl.ANY)
        smem = pl.BlockSpec(memory_space=pltpu.SMEM)
        vmem = pl.BlockSpec(memory_space=pltpu.VMEM)
        mixed_out, req_states, req_edges = pl.pallas_call(
            kernel,
            out_shape=(
                jax.ShapeDtypeStruct((rc, D), BF16),
                jax.ShapeDtypeStruct((NR, N, E), F32),
                jax.ShapeDtypeStruct((J, NR, E), F32),
            ),
            in_specs=[anyspec] * 16 + [smem] * 2,
            out_specs=(vmem,) * 3,
            scratch_shapes=list(scratch.values()),
            compiler_params=pltpu.CompilerParams(
                collective_id=0, has_side_effects=True, vmem_limit_bytes=58 * 2**20
            ),
        )(*[arrays[k] for k in NAMES], prompt_lengths, request_prompt)
        return mixed_out, req_states, jnp.transpose(req_edges.astype(BF16), (1, 0, 2))

    return local


def solution(mesh):
    placed = (
        P("seq", None),
        P(),
        P(None, "tp"),
        P(None, "tp"),
        P(None, "tp"),
        P("tp"),
        P("tp", None),
        P(None, "tp"),
        P("tp"),
        P(None, "tp"),
        P("tp"),
        P("tp", None),
        P(),
        P(None, "tp"),
        P(None, "tp"),
        P("tp", None),
        P(),
        P("seq"),
    )
    return jax.shard_map(
        make_local(mesh.shape["seq"], mesh.shape["tp"]),
        mesh=mesh,
        in_specs=placed,
        out_specs=(P(("seq", "tp"), None), P("seq", None, "tp"), P("seq", None, "tp")),
        check_vma=False,
    )
```

```python
import jax
import jax.numpy as jnp
from jax import lax
from jax.experimental import pallas as pl
from jax.experimental.pallas import tpu as pltpu
from jax.sharding import PartitionSpec as P

EPSILON = 1e-05
F32 = jnp.float32
BF16 = jnp.bfloat16
FAR = 1e30
GROUP = 8


def rms_norm(values, gain):
    scale = lax.rsqrt(jnp.mean(values * values, axis=-1, keepdims=True) + EPSILON)
    return values * scale * gain


def silu(v):
    return v * jax.nn.sigmoid(v)


def dot(a, b):
    return jnp.dot(a, b, preferred_element_type=F32)


def remote(src, dst, send_sem, recv_sem, device):
    return pltpu.make_async_remote_copy(
        src_ref=src,
        dst_ref=dst,
        send_sem=send_sem,
        recv_sem=recv_sem,
        device_id=device,
        device_id_type=pl.DeviceIdType.MESH,
    )


NAMES = (
    "tokens", "norm_gain", "w_x", "w_z", "conv_w", "conv_b", "w_xproj", "w_dt", "dt_bias",
    "a_log", "d_skip", "w_out", "mlp_gain", "w_gate", "w_up", "w_down",
)
EARLY = NAMES[:3]
LATE = ("w_out", "w_gate", "w_up", "w_down")
NEXT = tuple(k for k in NAMES if k not in EARLY + LATE)


def make_local(S, T):
    X = T // 2

    def local(*args):
        arrays = dict(zip(NAMES, args[:16]))
        prompt_lengths, request_prompt = args[16:]
        for k in ("norm_gain", "conv_b", "dt_bias", "d_skip", "mlp_gain"):
            arrays[k] = arrays[k][None, :]
        B, D = arrays["tokens"].shape
        E = arrays["w_x"].shape[1]
        K = arrays["conv_w"].shape[0]
        R = arrays["w_dt"].shape[0]
        N = arrays["a_log"].shape[0]
        M = arrays["w_xproj"].shape[1]
        arrays["w_xproj"] = arrays["w_xproj"].T
        FF = arrays["w_gate"].shape[1]
        NP = prompt_lengths.shape[0]
        NR = request_prompt.shape[0]
        rc = B // T
        J = K - 1
        EP = -(-NP * J // 16) * 16
        FR = NP * N + EP
        groups = B // GROUP
        cw = min(D, 512)
        CH = D // cw

        scratch = {k: pltpu.VMEM(arrays[k].shape, arrays[k].dtype) for k in NAMES}
        scratch.update(
            load_sem=pltpu.SemaphoreType.DMA((16,)),
            edge_s=pltpu.VMEM((16, E), BF16),
            edge_r=pltpu.VMEM((16, E), BF16),
            edge_sem=pltpu.SemaphoreType.DMA((2,)),
            ext=pltpu.VMEM((8 + B, E), F32),
            z=pltpu.VMEM((B, E), F32),
            pj=pltpu.VMEM((T, B, M), BF16),
            pj_send=pltpu.SemaphoreType.DMA((T,)),
            pj_recv=pltpu.SemaphoreType.DMA((T,)),
            mp=pltpu.VMEM((B, 256), F32),
            m3=pltpu.VMEM((groups, 2 * N, GROUP), F32),
            stepd=pltpu.VMEM((B, E), F32),
            drv=pltpu.VMEM((B, E), F32),
            dec=pltpu.VMEM((B, N, E), F32),
            sts=pltpu.VMEM((B, N, E), F32),
            y=pltpu.VMEM((B, E), F32),
            ssum=pltpu.VMEM((S, 1, E), F32),
            sbuf=pltpu.VMEM((S, N, E), BF16),
            a_send=pltpu.SemaphoreType.DMA((S,)),
            a_recv=pltpu.SemaphoreType.DMA((S,)),
            b_send=pltpu.SemaphoreType.DMA((S,)),
            b_recv=pltpu.SemaphoreType.DMA((S,)),
            fin=pltpu.VMEM((S, FR, E), BF16),
            f_send=pltpu.SemaphoreType.DMA((S,)),
            f_recv=pltpu.SemaphoreType.DMA((S,)),
            stat=pltpu.VMEM((NP, N, E), F32),
            edg=pltpu.VMEM((NP, 8, E), F32),
            part=pltpu.VMEM((CH, 2, X, rc, cw), BF16),
            recv1=pltpu.VMEM((CH, X, rc, cw), BF16),
            psb=pltpu.VMEM((CH, X, rc, cw), BF16),
            recv2=pltpu.VMEM((X, CH, X, rc, cw), BF16),
            res=pltpu.VMEM((X, rc, D), F32),
            n2=pltpu.VMEM((2, X, rc, D), BF16),
            hid=pltpu.VMEM((B, FF), BF16),
            partb=pltpu.VMEM((CH, 2, X, rc, cw), BF16),
            recv3=pltpu.VMEM((CH, X, rc, cw), BF16),
            psb2=pltpu.VMEM((CH, X, rc, cw), BF16),
            recv4=pltpu.VMEM((X, CH, rc, cw), BF16),
            swap_sem=pltpu.SemaphoreType.DMA((2,)),
            c_send=pltpu.SemaphoreType.DMA((2, CH)),
            c_recv=pltpu.SemaphoreType.DMA((2, CH)),
            x_send=pltpu.SemaphoreType.DMA((2, CH, X)),
            x_recv=pltpu.SemaphoreType.DMA((2, CH, X)),
        )
        keys = list(scratch)

        def kernel(*refs):
            hbm = dict(zip(NAMES, refs[:16]))
            lens, reqs, out, out_states, out_edges = refs[16:21]
            s = dict(zip(keys, refs[21:]))
            seq = lax.axis_index("seq")
            tp = lax.axis_index("tp")
            x = lax.div(tp, 2)
            c = lax.rem(tp, 2)
            sib = {"tp": x * 2 + 1 - c}

            loads = {
                k: pltpu.make_async_copy(hbm[k], s[k], s["load_sem"].at[i])
                for i, k in enumerate(NAMES)
            }
            for k in EARLY:
                loads[k].start()

            barrier = pltpu.get_barrier_semaphore()
            for i in range(1, T):
                pl.semaphore_signal(
                    barrier, 1, device_id={"tp": lax.rem(tp + i, T)},
                    device_id_type=pl.DeviceIdType.MESH,
                )

            @pl.loop(1, S)
            def _(i):
                pl.semaphore_signal(
                    barrier, 1, device_id={"seq": lax.rem(seq + i, S)},
                    device_id_type=pl.DeviceIdType.MESH,
                )

            for k in NEXT:
                loads[k].start()

            ends, starts = [], []
            total = jnp.int32(0)
            for p in range(NP):
                starts.append(total)
                total = total + lens[p]
                ends.append(total)
            first = seq * B
            places = first + lax.broadcasted_iota(jnp.int32, (B, 1), 0)
            start_of = jnp.zeros((B, 1), jnp.int32)
            begins = jnp.zeros((B, 1), jnp.int32)
            for p in range(NP):
                here = (places >= starts[p]) & (places < ends[p])
                start_of = jnp.where(here, starts[p], start_of)
                begins = jnp.where(places == starts[p], 1, begins)
            offset = places - start_of

            loads["tokens"].wait()
            loads["norm_gain"].wait()
            normed = rms_norm(s["tokens"][...].astype(F32), s["norm_gain"][...]).astype(BF16)
            loads["w_x"].wait()
            for k in LATE:
                loads[k].start()
            xb = dot(normed, s["w_x"][...]).astype(BF16)
            s["edge_s"][...] = xb[B - 16 :]
            xf = xb.astype(F32)
            s["ext"][8:, :] = xf
            pl.semaphore_wait(barrier, T - 1 + S - 1)
            edge = remote(
                s["edge_s"], s["edge_r"], s["edge_sem"].at[0], s["edge_sem"].at[1],
                {"seq": lax.rem(seq + 1, S)},
            )

            @pl.when(seq < S - 1)
            def _():
                edge.start()

            for k in NEXT:
                loads[k].wait()
            half = E // 2
            s["z"][:, :half] = dot(normed, s["w_z"][:, :half])

            @pl.when(seq > 0)
            def _():
                edge.wait_recv()
                s["ext"][0:8, :] = s["edge_r"][...].astype(F32)[8:]

            @pl.when(seq == 0)
            def _():
                s["ext"][0:8, :] = jnp.zeros((8, E), F32)

            acc = jnp.zeros((B, E), F32) + s["conv_b"][...]
            for lag in range(K):
                window = s["ext"][8 - lag : 8 - lag + B, :]
                mask = jnp.where(offset >= lag, 1.0, 0.0)
                acc = acc + s["conv_w"][J - lag : J - lag + 1, :] * window * mask
            conv_out = silu(acc).astype(BF16)

            s["pj"][0] = lax.dot_general(
                conv_out, s["w_xproj"][...], (((1,), (1,)), ((), ())),
                preferred_element_type=F32,
            ).astype(BF16)
            pj = []
            for i in range(1, T):
                pj.append(
                    remote(
                        s["pj"].at[0], s["pj"].at[i], s["pj_send"].at[i], s["pj_recv"].at[i],
                        {"tp": lax.rem(tp + i, T)},
                    )
                )
                pj[-1].start()
            s["z"][:, half:] = dot(normed, s["w_z"][:, half:])
            rates = -jnp.exp(s["a_log"][...])
            conv = conv_out.astype(F32)
            s["mp"][...] = jnp.zeros((B, 256), F32)
            projected = s["pj"][0].astype(F32)
            for i in range(1, T):
                pj[i - 1].wait_recv()
                projected = projected + s["pj"][i].astype(F32)
            s["mp"][:, :M] = projected
            maps = jnp.transpose(s["mp"][:, R : R + 128])
            for g in range(groups):
                s["m3"][g] = maps[: 2 * N, g * GROUP : (g + 1) * GROUP]
            low = s["mp"][:, :R].astype(BF16)
            pre = dot(low, s["w_dt"][...]) + s["dt_bias"][...]
            step = jnp.maximum(pre, 0.0) + jnp.log1p(jnp.exp(-jnp.abs(pre)))
            s["drv"][...] = step * conv
            stepd = jnp.where(begins > 0, FAR, step)
            s["stepd"][...] = stepd
            s["ssum"][seq] = jnp.sum(stepd, axis=0, keepdims=True)

            def send_a(d):
                return remote(
                    s["ssum"].at[seq], s["ssum"].at[seq], s["a_send"].at[d],
                    s["a_recv"].at[seq], {"seq": d},
                )

            def send_b(d):
                return remote(
                    s["sbuf"].at[seq], s["sbuf"].at[seq], s["b_send"].at[d],
                    s["b_recv"].at[seq], {"seq": d},
                )

            @pl.loop(seq + 1, S)
            def _(d):
                send_a(d).start()

            def one(g, st):
                base = pl.multiple_of(g * GROUP, GROUP)
                sg = s["stepd"][pl.ds(base, GROUP), :]
                dg = s["drv"][pl.ds(base, GROUP), :]
                mg = s["m3"][g]
                for i in range(GROUP):
                    decay = jnp.exp(sg[i : i + 1, :] * rates)
                    s["dec"][base + i] = decay
                    st = decay * st + dg[i : i + 1, :] * mg[:N, i : i + 1]
                return st

            last = lax.fori_loop(0, groups, one, jnp.zeros((N, E), F32))
            s["sbuf"][seq] = last.astype(BF16)

            @pl.loop(seq + 1, S)
            def _(d):
                send_b(d).start()

            s["z"][...] = silu(s["z"][...].astype(BF16).astype(F32))

            def join(e, st):
                remote(
                    s["ssum"].at[e], s["ssum"].at[e], s["a_send"].at[e], s["a_recv"].at[e],
                    {"seq": e},
                ).wait_recv()
                remote(
                    s["sbuf"].at[e], s["sbuf"].at[e], s["b_send"].at[e], s["b_recv"].at[e],
                    {"seq": e},
                ).wait_recv()
                return jnp.exp(s["ssum"][e] * rates) * st + s["sbuf"][e].astype(F32)

            state_in = lax.fori_loop(0, seq, join, jnp.zeros((N, E), F32))

            def two(g, st):
                base = pl.multiple_of(g * GROUP, GROUP)
                dg = s["drv"][pl.ds(base, GROUP), :]
                mg = s["m3"][g]
                rows = []
                for i in range(GROUP):
                    st = s["dec"][base + i] * st + dg[i : i + 1, :] * mg[:N, i : i + 1]
                    s["sts"][base + i] = st
                    rows.append(jnp.sum(st * mg[N:, i : i + 1], axis=0, keepdims=True))
                s["y"][pl.ds(base, GROUP), :] = jnp.concatenate(rows, axis=0)
                return st

            lax.fori_loop(0, groups, two, state_in)
            gated = ((s["y"][...] + s["d_skip"][...] * conv) * s["z"][...]).astype(BF16)

            loads["w_out"].wait()
            s["hid"][:, :E] = gated
            sums = ([], [])
            over_x = ([], [])

            def chunk(j):
                return slice(j * cw, (j + 1) * cw)

            def in_chip(k, j, left, w, dest, land, place_of):
                val = dot(left, w[:, chunk(j)]).astype(BF16)
                for q in range(T):
                    cc, xx = place_of(q)
                    dest[j, cc, xx] = val[q * rc : (q + 1) * rc]
                r = remote(
                    dest.at[j, 1 - c], land.at[j], s["c_send"].at[k, j], s["c_recv"].at[k, j], sib
                )
                r.start()
                sums[k].append(r)

            def pair_sum(k, j, part, land, dest):
                sums[k][j].wait_recv()
                dest[j] = (part[j, c].astype(F32) + land[j].astype(F32)).astype(BF16)
                for i in range(1, X):
                    there = lax.rem(x + i, X)
                    r = remote(
                        dest.at[j] if k == 0 else dest.at[j, there],
                        s["recv2" if k == 0 else "recv4"].at[i, j],
                        s["x_send"].at[k, j, i],
                        s["x_recv"].at[k, j, i],
                        {"tp": there * 2 + c},
                    )
                    r.start()
                    over_x[k].append(r)

            for j in range(CH + 1):
                if j < CH:
                    in_chip(
                        0, j, s["hid"][:, :E], s["w_out"], s["part"], s["recv1"],
                        lambda q: (q % 2, q // 2),
                    )
                if j > 0:
                    pair_sum(0, j - 1, s["part"], s["recv1"], s["psb"])

            for p in range(NP):
                row = jnp.clip(ends[p] - 1 - first, 0, B - 1)
                s["fin"][seq, p * N : (p + 1) * N, :] = s["sts"][row].astype(BF16)
            rows = []
            for p in range(NP):
                for j in range(J):
                    target = jnp.clip(ends[p] - J + j - first + 8, 0, B + 7)
                    got = s["ext"][pl.ds(target, 1), :]
                    rows.append(jnp.where(ends[p] - J + j >= starts[p], got, 0.0))
            rows += [jnp.zeros((1, E), F32)] * (EP - NP * J)
            s["fin"][seq, NP * N :, :] = jnp.concatenate(rows, axis=0).astype(BF16)

            def send_f(i):
                return remote(
                    s["fin"].at[seq], s["fin"].at[seq], s["f_send"].at[i], s["f_recv"].at[seq],
                    {"seq": lax.rem(seq + i, S)},
                )

            @pl.loop(1, S)
            def _(i):
                send_f(i).start()

            for j in range(CH):
                for i in range(1, X):
                    over_x[0][j * (X - 1) + i - 1].wait_recv()
                for b in range(X):
                    at = pl.ds(pl.multiple_of((2 * b + c) * rc, rc), rc)
                    val = s["tokens"][at, chunk(j)].astype(F32) + s["psb"][j, b].astype(F32)
                    for i in range(1, X):
                        val = val + s["recv2"][i, j, b].astype(F32)
                    s["res"][b, :, chunk(j)] = val
            for b in range(X):
                s["n2"][c, b] = rms_norm(s["res"][b], s["mlp_gain"][...]).astype(BF16)
            swap = remote(
                s["n2"].at[c], s["n2"].at[c], s["swap_sem"].at[0], s["swap_sem"].at[1], sib
            )
            swap.start()
            for k in ("w_gate", "w_up", "w_down"):
                loads[k].wait()
            swap.wait_recv()

            wide = min(FF, 256)

            @pl.loop(0, FF // wide)
            def _(j):
                at = pl.ds(pl.multiple_of(j * wide, wide), wide)
                left = s["n2"][...].reshape(B, D)
                gate = dot(left, s["w_gate"][:, at])
                up = dot(left, s["w_up"][:, at])
                s["hid"][:, at] = (silu(gate) * up).astype(BF16)

            for j in range(CH + 1):
                if j < CH:
                    in_chip(
                        1, j, s["hid"][...], s["w_down"], s["partb"], s["recv3"],
                        lambda q: (q // X, q % X),
                    )
                if j > 0:
                    pair_sum(1, j - 1, s["partb"], s["recv3"], s["psb2"])

            @pl.loop(1, S)
            def _(i):
                e = lax.rem(seq + i, S)
                remote(
                    s["fin"].at[e], s["fin"].at[e], s["f_send"].at[i], s["f_recv"].at[e],
                    {"seq": e},
                ).wait_recv()

            for p in range(NP):
                owner = lax.div(ends[p] - 1, B)
                got = s["fin"][owner]
                s["stat"][p] = got[p * N : (p + 1) * N].astype(F32)
                s["edg"][p, 0:J, :] = got[NP * N :].astype(F32)[p * J : (p + 1) * J]
            for r in range(NR):
                out_states[r] = s["stat"][reqs[r]]
                picked = s["edg"][reqs[r]]
                for j in range(J):
                    out_edges[j, r : r + 1, :] = picked[j : j + 1]

            slot = first + tp * rc + lax.broadcasted_iota(jnp.int32, (rc, 1), 0)
            live = jnp.where(slot < total, 1.0, 0.0)
            for j in range(CH):
                val = s["res"][x, :, chunk(j)] + s["psb2"][j, x].astype(F32)
                for i in range(1, X):
                    over_x[1][j * (X - 1) + i - 1].wait_recv()
                    val = val + s["recv4"][i, j].astype(F32)
                out[:, chunk(j)] = (val * live).astype(BF16)

            @pl.when(seq < S - 1)
            def _():
                edge.wait_send()

            for r in pj + over_x[0] + over_x[1] + sums[0] + sums[1] + [swap]:
                r.wait_send()

            @pl.loop(seq + 1, S)
            def _(d):
                send_a(d).wait_send()
                send_b(d).wait_send()

            @pl.loop(1, S)
            def _(i):
                send_f(i).wait_send()

        anyspec = pl.BlockSpec(memory_space=pl.ANY)
        smem = pl.BlockSpec(memory_space=pltpu.SMEM)
        vmem = pl.BlockSpec(memory_space=pltpu.VMEM)
        mixed_out, req_states, req_edges = pl.pallas_call(
            kernel,
            out_shape=(
                jax.ShapeDtypeStruct((rc, D), BF16),
                jax.ShapeDtypeStruct((NR, N, E), F32),
                jax.ShapeDtypeStruct((J, NR, E), F32),
            ),
            in_specs=[anyspec] * 16 + [smem] * 2,
            out_specs=(vmem,) * 3,
            scratch_shapes=list(scratch.values()),
            compiler_params=pltpu.CompilerParams(
                collective_id=0, has_side_effects=True, vmem_limit_bytes=58 * 2**20
            ),
        )(*[arrays[k] for k in NAMES], prompt_lengths, request_prompt)

        def hand_over(mixed_in, states_in, edges_in, mixed, states, edges, sem):
            copies = [
                pltpu.make_async_copy(mixed_in, mixed, sem.at[0]),
                pltpu.make_async_copy(states_in, states, sem.at[1]),
            ]
            for copy in copies:
                copy.start()
            edges[...] = edges_in[...].astype(BF16)
            for copy in copies:
                copy.wait()

        mixed_out, req_states, req_edges = pl.pallas_call(
            hand_over,
            out_shape=(
                jax.ShapeDtypeStruct((rc, D), BF16),
                jax.ShapeDtypeStruct((NR, N, E), F32),
                jax.ShapeDtypeStruct((J, NR, E), BF16),
            ),
            in_specs=[anyspec, anyspec, vmem],
            out_specs=(anyspec, anyspec, vmem),
            scratch_shapes=[pltpu.SemaphoreType.DMA((2,))],
        )(mixed_out, req_states, req_edges)
        return mixed_out, req_states, jnp.transpose(req_edges, (1, 0, 2))

    return local


def solution(mesh):
    placed = (
        P("seq", None),
        P(),
        P(None, "tp"),
        P(None, "tp"),
        P(None, "tp"),
        P("tp"),
        P("tp", None),
        P(None, "tp"),
        P("tp"),
        P(None, "tp"),
        P("tp"),
        P("tp", None),
        P(),
        P(None, "tp"),
        P(None, "tp"),
        P("tp", None),
        P(),
        P("seq"),
    )
    return jax.shard_map(
        make_local(mesh.shape["seq"], mesh.shape["tp"]),
        mesh=mesh,
        in_specs=placed,
        out_specs=(P(("seq", "tp"), None), P("seq", None, "tp"), P("seq", None, "tp")),
        check_vma=False,
    )
```
